32 devices in a mesh: fus: 8 (over z, x), blade: 4 (over y, core).
Axes of the slice: x: 2, y: 2, z: 4, core: 2. Of those that a mesh axis runs over, the one named last changes fastest.
Arguments:
- airframe_coords: float32 [3, 2048], P(None, 'fus'), may hold values from -6 to 6
- airframe_normals: float32 [3, 2048], P(None, 'fus'), may hold values from -6 to 6
- airframe_strength: float32 [4, 2048], P(None, 'fus'), may hold values from -6 to 6
- blade_coords: float32 [4, 3, 16384], P(None, None, ('fus', 'blade')), may hold values from -6 to 6
- blade_strength: float32 [4, 16384], P(None, ('fus', 'blade')), may hold values from -6 to 6
- blade_index: int32 [16384], P(('fus', 'blade')), may hold values from 0 to 3
- azimuth: float32 [4], replicated, may hold values from -3.140625 to 3.140625
- onset: float32 [3], replicated, may hold values from -4 to 4
Outputs:
- normal_velocity: float32 [4, 2048], P(None, ('fus', 'blade'))
- blade_velocity: float32 [4, 3, 16384], P(None, None, ('fus', 'blade'))
- residual: float32 [4, 2048], P(None, ('fus', 'blade'))
The draws below stay inside these ranges and needn't reach their ends.
All inputs are finite; a program needn't handle non-finite values.
Results may differ from the reference program's by a relative error of at most 0.0001.
Values sent between devices are 32-bit elements; how exact they have to be, the bound alone decides.
A program may use at most 64 MiB of HBM per device.

```python
import math
import jax
import jax.numpy as jnp
from jax import lax

SUBSTEPS = 4
NF = 2048
NB = 16384


def draw_airframe_coords(key, part):
    key = jax.random.fold_in(key, 11)
    unit = jax.random.uniform(key, (3, NF), jnp.float32)
    across = 12.0 * unit[:2] - 6.0
    height = -6.0 * unit[2]
    return jnp.concatenate([across, height[None, :]], axis=0).astype(jnp.float32)


def draw_blade_coords(key, part):
    key = jax.random.fold_in(key, 23)
    unit = jax.random.uniform(key, (SUBSTEPS, 3, NB), jnp.float32)
    across = 4.2 * (2.0 * unit[:, :2] - 1.0)
    height = 0.5 + 5.5 * unit[:, 2]
    return jnp.concatenate([across, height[:, None, :]], axis=1).astype(jnp.float32)


def plant(drawn, own_key, least, top_value):
    index_at = [jax.random.randint(jax.random.fold_in(own_key, axis), (), 0, length) for axis, length in enumerate(drawn.shape)]
    longest = drawn.shape.index(max(drawn.shape))
    neighbour = index_at[:longest] + [(index_at[longest] + 1) % drawn.shape[longest]] + index_at[longest + 1:]
    return drawn.at[tuple(index_at)].set(least).at[tuple(neighbour)].set(top_value)


def level_of(rng, dims, shards, low, top_value):
    def one(axis_at, blocks):
        draws = jax.random.uniform(jax.random.fold_in(jax.random.fold_in(rng, 6), axis_at), (blocks,), jnp.float32, low / len(shards), top_value / len(shards))
        return jnp.repeat(jnp.exp(draws), dims[axis_at] // blocks).reshape((-1,) + (1,) * (len(dims) - axis_at - 1))

    gain = one(*shards[0])
    for cut in shards[1:]:
        gain = gain * one(*cut)
    return gain


def centred(rng, dims, spread, reach, shards=(), held_as=jnp.bfloat16):
    array = spread * jax.random.normal(rng, dims, jnp.float32)
    if shards:
        array = array * level_of(rng, dims, shards, -0.22, 0.18)
    return jnp.clip(array, -reach, reach).astype(held_as)


def setup_inputs(seed: int = 0) -> dict:
    splits = jax.random.split(jax.random.key(seed), 9)
    airframe_coords = draw_airframe_coords(jax.random.fold_in(splits[8], 71), 0)
    airframe_normals = centred(splits[1], (3, NF), 1.0, 6.0, ((1, 8),), jnp.float32)
    airframe_strength = centred(splits[2], (SUBSTEPS, NF), 1.0, 6.0, ((1, 8),), jnp.float32)
    blade_coords = draw_blade_coords(jax.random.fold_in(splits[8], 71), 0)
    blade_strength = centred(splits[4], (SUBSTEPS, NB), 1.0, 6.0, ((1, 32),), jnp.float32)
    blade_index = plant(jax.random.randint(splits[5], (NB,), 0, 4), jax.random.fold_in(splits[5], 1), 0, 3).astype(jnp.int32)
    azimuth = jnp.clip(jax.random.uniform(splits[6], (SUBSTEPS,), jnp.float32, -3.140625, 3.140625), -3.140625, 3.140625)
    onset = centred(splits[7], (3,), 1.0, 4.0, (), jnp.float32)
    return {"airframe_coords": airframe_coords, "airframe_normals": airframe_normals, "airframe_strength": airframe_strength, "blade_coords": blade_coords, "blade_strength": blade_strength, "blade_index": blade_index, "azimuth": azimuth, "onset": onset}


core_sq = 0.01
kernel_scale = 1.0 / (4.0 * math.pi)

def rotate(blade_coords, blade_index, azimuth):
    angle = azimuth[:, None] + blade_index.astype(jnp.float32)[None, :] * (math.pi / 2.0)
    cosine = jnp.cos(angle)
    sine = jnp.sin(angle)
    return jnp.stack([cosine * blade_coords[:, 0] - sine * blade_coords[:, 1], sine * blade_coords[:, 0] + cosine * blade_coords[:, 1], blade_coords[:, 2]], axis=1)

def tile_terms(frame_pos, frame_norm, frame_str, blade_pos, blade_str):
    delta_x = frame_pos[0][:, None] - blade_pos[0][None, :]
    delta_y = frame_pos[1][:, None] - blade_pos[1][None, :]
    delta_z = frame_pos[2][:, None] - blade_pos[2][None, :]
    dist_sq = delta_x * delta_x + delta_y * delta_y + delta_z * delta_z + core_sq
    weight = kernel_scale * lax.rsqrt(dist_sq) / dist_sq
    projected = frame_norm[0][:, None] * delta_x + frame_norm[1][:, None] * delta_y + frame_norm[2][:, None] * delta_z
    normal_term = lax.optimization_barrier(jnp.sum(weight * projected * blade_str[None, :], axis=1))
    scaled = weight * frame_str[:, None]
    blade_term = -jnp.stack([lax.optimization_barrier(jnp.sum(scaled * delta_x, 0)), lax.optimization_barrier(jnp.sum(scaled * delta_y, 0)), lax.optimization_barrier(jnp.sum(scaled * delta_z, 0))])
    return (normal_term, blade_term)

def reference(airframe_coords, airframe_normals, airframe_strength, blade_coords, blade_strength, blade_index, azimuth, onset):
    blade_pos = rotate(blade_coords, blade_index, azimuth)
    rows = 64 if NF % 64 == 0 else NF
    count = NF // rows
    pos_blocks = jnp.transpose(airframe_coords.reshape(3, count, rows), (1, 0, 2))
    norm_blocks = jnp.transpose(airframe_normals.reshape(3, count, rows), (1, 0, 2))

    def substep(inputs):
        frame_str, bpos, bstr = inputs
        str_blocks = frame_str.reshape(count, rows)

        def step_fn(carry, block):
            normal_term, blade_term = tile_terms(block[0], block[1], block[2], bpos, bstr)
            return (carry + blade_term, normal_term)
        blade_vel, normal_blocks = lax.scan(step_fn, jnp.zeros((3, NB), jnp.float32), (pos_blocks, norm_blocks, str_blocks))
        return (normal_blocks.reshape(NF), blade_vel)
    normal_velocity, blade_velocity = lax.map(substep, (airframe_strength, blade_pos, blade_strength))
    onset_part = airframe_normals[0] * onset[0] + airframe_normals[1] * onset[1] + airframe_normals[2] * onset[2]
    residual = normal_velocity + onset_part[None, :] + 0.5 * airframe_strength
    return (normal_velocity, blade_velocity, residual)
```

```python
import functools
import math

import jax
import jax.numpy as jnp
from jax import lax
from jax.experimental import pallas as pl
from jax.experimental.pallas import tpu as pltpu
from jax.sharding import PartitionSpec as P

core_sq = 0.01
kernel_scale = 1.0 / (4.0 * math.pi)
MESH = pl.DeviceIdType.MESH
F32 = jnp.float32
BF16 = jnp.bfloat16
LANES = 128
ROWS = 16


def split3(value):
    high = value.astype(BF16).astype(F32)
    rest = value - high
    mid = rest.astype(BF16).astype(F32)
    low = (rest - mid).astype(BF16).astype(F32)
    return jnp.concatenate([high, mid, low, jnp.zeros_like(value)], axis=0).astype(BF16)


def fold3(parts):
    pair = parts[0:8] + parts[8:16]
    return pair[0:4] + pair[4:8]


def kernel(
    n, nb,
    ac_ref, an_ref, aq_ref, bc_ref, bs_ref, bi_ref, az_ref, on_ref,
    nv_ref, bv_ref, rs_ref,
    gath, spread, pos, yparts, xparts, whi, wlo, acc, stage, land,
    g_send, g_recv, p_send, p_recv,
):
    steps = bc_ref.shape[0]
    width = bc_ref.shape[2]
    frame = ac_ref.shape[1]
    quarter = frame // nb
    per_chunk = LANES // quarter
    me_f = lax.axis_index("fus")
    me_b = lax.axis_index("blade")

    barrier = pltpu.get_barrier_semaphore()

    def greet(i, _):
        other = lax.rem(me_f * nb + me_b + i, n * nb)
        pl.semaphore_signal(
            barrier, inc=1, device_id=(other // nb, lax.rem(other, nb)), device_id_type=MESH
        )
        return 0

    lax.fori_loop(1, n * nb, greet, 0)

    gath[0, 0:3, :] = ac_ref[...]
    gath[0, 3:6, :] = an_ref[...]
    gath[0, 6 : 6 + steps, :] = aq_ref[...]

    row = lax.broadcasted_iota(jnp.int32, (steps, width), 0)
    azimuth = jnp.zeros((steps, width), F32)
    for s in range(steps):
        azimuth = jnp.where(row == s, az_ref[s], azimuth)
    angle = azimuth + bi_ref[...].astype(F32) * (math.pi / 2.0)
    cosine = jnp.cos(angle)
    sine = jnp.sin(angle)
    x = bc_ref[:, 0, :]
    y = bc_ref[:, 1, :]
    pos[0] = cosine * x - sine * y
    pos[1] = sine * x + cosine * y
    pos[2] = bc_ref[:, 2, :]
    for s in range(steps):
        strength = bs_ref[s : s + 1, :]
        yparts[s] = split3(
            jnp.concatenate(
                [strength] + [strength * pos[c, s : s + 1, :] for c in range(3)], axis=0
            )
        )
    acc[...] = jnp.zeros_like(acc)

    pl.semaphore_wait(barrier, n * nb - 1)

    def send_frame(k, _):
        other = lax.rem(me_f + n - k, n)
        pltpu.make_async_remote_copy(
            src_ref=gath.at[0],
            dst_ref=gath.at[k],
            send_sem=g_send,
            recv_sem=g_recv.at[k],
            device_id=(other, me_b),
            device_id_type=MESH,
        ).start()
        return 0

    lax.fori_loop(1, n, send_frame, 0)

    for s in range(steps):
        for c in range(3):
            for j in range(width // LANES):
                piece = pos[c, s : s + 1, j * LANES : (j + 1) * LANES]
                spread[s * 3 + c, j * LANES : (j + 1) * LANES, :] = jnp.broadcast_to(
                    piece, (LANES, LANES)
                ).T

    def send_part(k, dest_f, dest_b, chunk):
        pltpu.make_async_remote_copy(
            src_ref=stage.at[k, chunk],
            dst_ref=land.at[k * nb + me_b],
            send_sem=p_send,
            recv_sem=p_recv,
            device_id=(dest_f, dest_b),
            device_id_type=MESH,
        ).start()

    def block(k, _):
        owner = lax.rem(me_f + k, n)

        @pl.when(k > 0)
        def _():
            pltpu.make_async_copy(gath.at[k], gath.at[k], g_recv.at[k]).wait()

        fx = gath[k, 0:1, :]
        fy = gath[k, 1:2, :]
        fz = gath[k, 2:3, :]
        nx = gath[k, 3:4, :]
        ny = gath[k, 4:5, :]
        nz = gath[k, 5:6, :]
        fxb = jnp.broadcast_to(fx, (8, frame))
        fyb = jnp.broadcast_to(fy, (8, frame))
        fzb = jnp.broadcast_to(fz, (8, frame))
        fx16 = jnp.concatenate([fxb, fxb], axis=0)
        fy16 = jnp.concatenate([fyb, fyb], axis=0)
        fz16 = jnp.concatenate([fzb, fzb], axis=0)
        out_rows = []
        for s in range(steps):
            q = gath[k, 6 + s : 7 + s, :]
            xs = split3(jnp.concatenate([q, q * fx, q * fy, q * fz], axis=0))
            slot = s % 2
            for r in range(width // ROWS):
                lines = slice(r * ROWS, (r + 1) * ROWS)
                bx = spread[s * 3, lines, :]
                by = spread[s * 3 + 1, lines, :]
                bz = spread[s * 3 + 2, lines, :]
                for h in range(frame // LANES):
                    cols = slice(h * LANES, (h + 1) * LANES)
                    dx = fx16[:, cols] - bx
                    dy = fy16[:, cols] - by
                    dz = fz16[:, cols] - bz
                    inv = lax.rsqrt(dx * dx + dy * dy + dz * dz + core_sq)
                    weight = inv * inv * inv
                    high = weight.astype(BF16)
                    whi[slot, lines, cols] = high
                    wlo[slot, lines, cols] = (weight - high.astype(F32)).astype(BF16)
            ys = yparts[s]
            high = whi[slot]
            low = wlo[slot]
            sums = fold3(
                jnp.dot(ys, high, preferred_element_type=F32)
                + jnp.dot(ys, low, preferred_element_type=F32)
            )
            base = sums[0:1]
            out_rows.append(
                kernel_scale
                * (
                    nx * (fx * base - sums[1:2])
                    + ny * (fy * base - sums[2:3])
                    + nz * (fz * base - sums[3:4])
                )
            )
            over = (((1,), (1,)), ((), ()))
            acc[s] += lax.dot_general(xs, high, over, preferred_element_type=F32) + lax.dot_general(
                xs, low, over, preferred_element_type=F32
            )
        part = jnp.concatenate(out_rows, axis=0)
        for h in range(frame // LANES):
            stage[k, h] = part[:, h * LANES : (h + 1) * LANES]

        @pl.when(k > 0)
        def _():
            for c in range(nb):
                send_part(k, owner, c, c // per_chunk)

        @pl.when(k == 0)
        def _():
            for d in range(1, nb):
                c = lax.rem(me_b + d, nb)
                send_part(0, me_f, c, c // per_chunk)

        return 0

    lax.fori_loop(0, n, block, 0)

    chunk = me_b // per_chunk
    land[me_b] = stage[0, chunk]

    for s in range(steps):
        sums = fold3(acc[s])
        for c in range(3):
            bv_ref[s, c : c + 1, :] = kernel_scale * (
                pos[c, s : s + 1, :] * sums[0:1] - sums[c + 1 : c + 2]
            )

    own = pl.ds(pl.multiple_of(chunk * LANES, LANES), LANES)
    onset_part = (
        an_ref[0:1, own] * on_ref[0] + an_ref[1:2, own] * on_ref[1] + an_ref[2:3, own] * on_ref[2]
    )
    extra = onset_part + 0.5 * aq_ref[:, own]

    rest = land.at[pl.ds(1, n * nb - 1)]
    pltpu.make_async_copy(rest, rest, p_recv).wait()
    total = jnp.sum(land[...], axis=0)
    resid = total + extra
    which = lax.rem(me_b, per_chunk)
    nv = total[:, 0:quarter]
    rv = resid[:, 0:quarter]
    for i in range(1, per_chunk):
        cols = slice(i * quarter, (i + 1) * quarter)
        nv = jnp.where(which == i, total[:, cols], nv)
        rv = jnp.where(which == i, resid[:, cols], rv)
    nv_ref[...] = nv
    rs_ref[...] = rv

    pltpu.make_async_copy(rest, rest, p_send).wait()
    blocks = gath.at[pl.ds(1, n - 1)]
    pltpu.make_async_copy(blocks, blocks, g_send).wait()


def body(n, nb, ac, an, aq, bc, bs, bi, az, onset):
    steps, _, width = bc.shape
    frame = ac.shape[1]
    quarter = frame // nb
    vmem = pl.BlockSpec(memory_space=pltpu.VMEM)
    smem = pl.BlockSpec(memory_space=pltpu.SMEM)
    return pl.pallas_call(
        functools.partial(kernel, n, nb),
        out_shape=(
            jax.ShapeDtypeStruct((steps, quarter), F32),
            jax.ShapeDtypeStruct((steps, 3, width), F32),
            jax.ShapeDtypeStruct((steps, quarter), F32),
        ),
        in_specs=[vmem] * 6 + [smem] * 2,
        out_specs=(vmem, vmem, vmem),
        scratch_shapes=[
            pltpu.VMEM((n, 16, frame), F32),
            pltpu.VMEM((steps * 3, width, LANES), F32),
            pltpu.VMEM((3, steps, width), F32),
            pltpu.VMEM((steps, 16, width), BF16),
            pltpu.VMEM((16, frame), BF16),
            pltpu.VMEM((2, width, frame), BF16),
            pltpu.VMEM((2, width, frame), BF16),
            pltpu.VMEM((steps, 16, width), F32),
            pltpu.VMEM((n, frame // LANES, steps, LANES), F32),
            pltpu.VMEM((n * nb, steps, LANES), F32),
            pltpu.SemaphoreType.DMA,
            pltpu.SemaphoreType.DMA((n,)),
            pltpu.SemaphoreType.DMA,
            pltpu.SemaphoreType.DMA,
        ],
        compiler_params=pltpu.CompilerParams(
            collective_id=0, has_side_effects=True, vmem_limit_bytes=24 * 1024 * 1024
        ),
    )(ac, an, aq, bc, bs, bi.reshape(1, width), az, onset)


def solution(mesh):
    n = mesh.shape["fus"]
    nb = mesh.shape["blade"]
    both = ("fus", "blade")
    return jax.shard_map(
        functools.partial(body, n, nb),
        mesh=mesh,
        in_specs=(
            P(None, "fus"),
            P(None, "fus"),
            P(None, "fus"),
            P(None, None, both),
            P(None, both),
            P(both),
            P(),
            P(),
        ),
        out_specs=(P(None, both), P(None, None, both), P(None, both)),
        check_vma=False,
    )
```

```python
import functools
import math

import jax
import jax.numpy as jnp
from jax import lax
from jax.experimental import pallas as pl
from jax.experimental.pallas import tpu as pltpu
from jax.sharding import PartitionSpec as P

core_sq = 0.01
kernel_scale = 1.0 / (4.0 * math.pi)
MESH = pl.DeviceIdType.MESH
F32 = jnp.float32
BF16 = jnp.bfloat16
LANES = 128
ROWS = 16
PIECE = 256


def split3(value):
    high = value.astype(BF16).astype(F32)
    rest = value - high
    mid = rest.astype(BF16).astype(F32)
    low = (rest - mid).astype(BF16).astype(F32)
    return jnp.concatenate([high, mid, low, jnp.zeros_like(value)], axis=0).astype(BF16)


def fold3(parts):
    pair = parts[0:8] + parts[8:16]
    return pair[0:4] + pair[4:8]


def kernel(
    n, nb,
    ac_ref, an_ref, aq_ref, bc_ref, bs_ref, bi_ref, az_ref, on_ref,
    nv_ref, bv_ref, rs_ref,
    gath, spread, pos, yparts, acc, stage, land,
    g_send, g_recv, p_send, p_recv,
):
    steps = bc_ref.shape[0]
    width = bc_ref.shape[2]
    frame = ac_ref.shape[1]
    quarter = frame // nb
    per_chunk = LANES // quarter
    me_f = lax.axis_index("fus")
    me_b = lax.axis_index("blade")

    barrier = pltpu.get_barrier_semaphore()

    def greet(i, _):
        other = lax.rem(me_f * nb + me_b + i, n * nb)
        pl.semaphore_signal(
            barrier, inc=1, device_id=(other // nb, lax.rem(other, nb)), device_id_type=MESH
        )
        return 0

    lax.fori_loop(1, n * nb, greet, 0)

    gath[0, 0:3, :] = ac_ref[...]
    gath[0, 3:6, :] = an_ref[...]
    gath[0, 6 : 6 + steps, :] = aq_ref[...]

    row = lax.broadcasted_iota(jnp.int32, (steps, width), 0)
    azimuth = jnp.zeros((steps, width), F32)
    for s in range(steps):
        azimuth = jnp.where(row == s, az_ref[s], azimuth)
    angle = azimuth + bi_ref[...].astype(F32) * (math.pi / 2.0)
    cosine = jnp.cos(angle)
    sine = jnp.sin(angle)
    x = bc_ref[:, 0, :]
    y = bc_ref[:, 1, :]
    pos[0] = cosine * x - sine * y
    pos[1] = sine * x + cosine * y
    pos[2] = bc_ref[:, 2, :]
    for s in range(steps):
        strength = bs_ref[s : s + 1, :]
        yparts[s] = split3(
            jnp.concatenate(
                [strength] + [strength * pos[c, s : s + 1, :] for c in range(3)], axis=0
            )
        )
    acc[...] = jnp.zeros_like(acc)

    pl.semaphore_wait(barrier, n * nb - 1)

    def send_frame(k, _):
        other = lax.rem(me_f + n - k, n)
        pltpu.make_async_remote_copy(
            src_ref=gath.at[0],
            dst_ref=gath.at[k],
            send_sem=g_send,
            recv_sem=g_recv.at[k],
            device_id=(other, me_b),
            device_id_type=MESH,
        ).start()
        return 0

    lax.fori_loop(1, n, send_frame, 0)

    for s in range(steps):
        for c in range(3):
            for j in range(width // LANES):
                piece = pos[c, s : s + 1, j * LANES : (j + 1) * LANES]
                spread[s * 3 + c, j * LANES : (j + 1) * LANES, :] = jnp.broadcast_to(
                    piece, (LANES, LANES)
                ).T

    def send_part(k, dest_f, dest_b, chunk):
        pltpu.make_async_remote_copy(
            src_ref=stage.at[k, chunk],
            dst_ref=land.at[k * nb + me_b],
            send_sem=p_send,
            recv_sem=p_recv,
            device_id=(dest_f, dest_b),
            device_id_type=MESH,
        ).start()

    def block(k, _):
        owner = lax.rem(me_f + k, n)

        @pl.when(k > 0)
        def _():
            pltpu.make_async_copy(gath.at[k], gath.at[k], g_recv.at[k]).wait()

        fx = gath[k, 0:1, :]
        fy = gath[k, 1:2, :]
        fz = gath[k, 2:3, :]
        nx = gath[k, 3:4, :]
        ny = gath[k, 4:5, :]
        nz = gath[k, 5:6, :]
        fxb = jnp.broadcast_to(fx, (8, frame))
        fyb = jnp.broadcast_to(fy, (8, frame))
        fzb = jnp.broadcast_to(fz, (8, frame))
        fx16 = jnp.concatenate([fxb, fxb], axis=0)
        fy16 = jnp.concatenate([fyb, fyb], axis=0)
        fz16 = jnp.concatenate([fzb, fzb], axis=0)
        xs = []
        for s in range(steps):
            q = gath[k, 6 + s : 7 + s, :]
            xs.append(split3(jnp.concatenate([q, q * fx, q * fy, q * fz], axis=0)))
        over = (((1,), (1,)), ((), ()))
        pieces = [(s, i) for s in range(steps) for i in range(width // PIECE)]
        held = [[[[] for _ in range(frame // LANES)] for _ in range(2)] for _ in pieces]
        sums = [None] * steps
        back = [None] * steps

        def fill(p, part):
            s, i = pieces[p]
            each = PIECE // ROWS // 4
            for r in range(part * each, (part + 1) * each):
                lines = slice(r * ROWS, (r + 1) * ROWS)
                source = slice(i * PIECE + r * ROWS, i * PIECE + (r + 1) * ROWS)
                bx = spread[s * 3, source, :]
                by = spread[s * 3 + 1, source, :]
                bz = spread[s * 3 + 2, source, :]
                for h in range(frame // LANES):
                    cols = slice(h * LANES, (h + 1) * LANES)
                    dx = fx16[:, cols] - bx
                    dy = fy16[:, cols] - by
                    dz = fz16[:, cols] - bz
                    inv = lax.rsqrt(dx * dx + dy * dy + dz * dz + core_sq)
                    weight = inv * inv * inv
                    high = weight.astype(BF16)
                    held[p][0][h].append(high)
                    held[p][1][h].append((weight - high.astype(F32)).astype(BF16))

        def dots(p, part):
            s, i = pieces[p]
            source = slice(i * PIECE, (i + 1) * PIECE)
            weight = jnp.concatenate(
                [jnp.concatenate(tall, axis=0) for tall in held[p][part % 2]], axis=1
            )
            if part < 2:
                term = jnp.dot(yparts[s, :, source], weight, preferred_element_type=F32)
                sums[s] = term if sums[s] is None else sums[s] + term
            else:
                term = lax.dot_general(xs[s], weight, over, preferred_element_type=F32)
                if part == 2:
                    back[s] = term
                else:
                    acc[s, :, source] += back[s] + term

        for p in range(len(pieces) + 1):
            for part in range(4):
                if p < len(pieces):
                    fill(p, part)
                if p > 0:
                    dots(p - 1, part)
        out_rows = []
        for s in range(steps):
            total = fold3(sums[s])
            base = total[0:1]
            out_rows.append(
                kernel_scale
                * (
                    nx * (fx * base - total[1:2])
                    + ny * (fy * base - total[2:3])
                    + nz * (fz * base - total[3:4])
                )
            )
        part = jnp.concatenate(out_rows, axis=0)
        for h in range(frame // LANES):
            stage[k, h] = part[:, h * LANES : (h + 1) * LANES]

        @pl.when(k > 0)
        def _():
            for c in range(nb):
                send_part(k, owner, c, c // per_chunk)

        @pl.when(k == 0)
        def _():
            for d in range(1, nb):
                c = lax.rem(me_b + d, nb)
                send_part(0, me_f, c, c // per_chunk)

        return 0

    lax.fori_loop(0, n, block, 0)

    chunk = me_b // per_chunk
    land[me_b] = stage[0, chunk]

    for s in range(steps):
        sums = fold3(acc[s])
        for c in range(3):
            bv_ref[s, c : c + 1, :] = kernel_scale * (
                pos[c, s : s + 1, :] * sums[0:1] - sums[c + 1 : c + 2]
            )

    own = pl.ds(pl.multiple_of(chunk * LANES, LANES), LANES)
    onset_part = (
        an_ref[0:1, own] * on_ref[0] + an_ref[1:2, own] * on_ref[1] + an_ref[2:3, own] * on_ref[2]
    )
    extra = onset_part + 0.5 * aq_ref[:, own]

    rest = land.at[pl.ds(1, n * nb - 1)]
    pltpu.make_async_copy(rest, rest, p_recv).wait()
    total = jnp.sum(land[...], axis=0)
    resid = total + extra
    which = lax.rem(me_b, per_chunk)
    nv = total[:, 0:quarter]
    rv = resid[:, 0:quarter]
    for i in range(1, per_chunk):
        cols = slice(i * quarter, (i + 1) * quarter)
        nv = jnp.where(which == i, total[:, cols], nv)
        rv = jnp.where(which == i, resid[:, cols], rv)
    nv_ref[...] = nv
    rs_ref[...] = rv

    pltpu.make_async_copy(rest, rest, p_send).wait()
    blocks = gath.at[pl.ds(1, n - 1)]
    pltpu.make_async_copy(blocks, blocks, g_send).wait()


def body(n, nb, ac, an, aq, bc, bs, bi, az, onset):
    steps, _, width = bc.shape
    frame = ac.shape[1]
    quarter = frame // nb
    vmem = pl.BlockSpec(memory_space=pltpu.VMEM)
    smem = pl.BlockSpec(memory_space=pltpu.SMEM)
    return pl.pallas_call(
        functools.partial(kernel, n, nb),
        out_shape=(
            jax.ShapeDtypeStruct((steps, quarter), F32),
            jax.ShapeDtypeStruct((steps, 3, width), F32),
            jax.ShapeDtypeStruct((steps, quarter), F32),
        ),
        in_specs=[vmem] * 6 + [smem] * 2,
        out_specs=(vmem, vmem, vmem),
        scratch_shapes=[
            pltpu.VMEM((n, 16, frame), F32),
            pltpu.VMEM((steps * 3, width, LANES), F32),
            pltpu.VMEM((3, steps, width), F32),
            pltpu.VMEM((steps, 16, width), BF16),
            pltpu.VMEM((steps, 16, width), F32),
            pltpu.VMEM((n, frame // LANES, steps, LANES), F32),
            pltpu.VMEM((n * nb, steps, LANES), F32),
            pltpu.SemaphoreType.DMA,
            pltpu.SemaphoreType.DMA((n,)),
            pltpu.SemaphoreType.DMA,
            pltpu.SemaphoreType.DMA,
        ],
        compiler_params=pltpu.CompilerParams(
            collective_id=0, has_side_effects=True, vmem_limit_bytes=24 * 1024 * 1024
        ),
    )(ac, an, aq, bc, bs, bi.reshape(1, width), az, onset)


def solution(mesh):
    n = mesh.shape["fus"]
    nb = mesh.shape["blade"]
    both = ("fus", "blade")
    return jax.shard_map(
        functools.partial(body, n, nb),
        mesh=mesh,
        in_specs=(
            P(None, "fus"),
            P(None, "fus"),
            P(None, "fus"),
            P(None, None, both),
            P(None, both),
            P(both),
            P(),
            P(),
        ),
        out_specs=(P(None, both), P(None, None, both), P(None, both)),
        check_vma=False,
    )
```

```python
import functools
import math

import jax
import jax.numpy as jnp
from jax import lax
from jax.experimental import pallas as pl
from jax.experimental.pallas import tpu as pltpu
from jax.sharding import PartitionSpec as P

core_sq = 0.01
kernel_scale = 1.0 / (4.0 * math.pi)
MESH = pl.DeviceIdType.MESH
F32 = jnp.float32
BF16 = jnp.bfloat16
LANES = 128
ROWS = 16
PIECE = 256


def split3(value):
    high = value.astype(BF16).astype(F32)
    rest = value - high
    mid = rest.astype(BF16).astype(F32)
    low = (rest - mid).astype(BF16).astype(F32)
    return jnp.concatenate([high, mid, low, jnp.zeros_like(value)], axis=0).astype(BF16)


def fold3(parts):
    pair = parts[0:8] + parts[8:16]
    return pair[0:4] + pair[4:8]


def kernel(
    n, nb,
    ac_ref, an_ref, aq_ref, bc_ref, bs_ref, bi_ref, az_ref, on_ref,
    nv_ref, bv_ref, rs_ref,
    gath, spread, pos, yparts, acc, stage, land,
    g_send, g_recv, p_send, p_recv,
):
    steps = bc_ref.shape[0]
    width = bc_ref.shape[2]
    frame = ac_ref.shape[1]
    quarter = frame // nb
    per_chunk = LANES // quarter
    me_f = lax.axis_index("fus")
    me_b = lax.axis_index("blade")

    barrier = pltpu.get_barrier_semaphore()

    def greet(i, _):
        other = lax.rem(me_f * nb + me_b + i, n * nb)
        pl.semaphore_signal(
            barrier, inc=1, device_id=(other // nb, lax.rem(other, nb)), device_id_type=MESH
        )
        return 0

    lax.fori_loop(1, n * nb, greet, 0)

    gath[0, 0:3, :] = ac_ref[...]
    gath[0, 3:6, :] = an_ref[...]
    gath[0, 6 : 6 + steps, :] = aq_ref[...]

    row = lax.broadcasted_iota(jnp.int32, (steps, width), 0)
    azimuth = jnp.zeros((steps, width), F32)
    for s in range(steps):
        azimuth = jnp.where(row == s, az_ref[s], azimuth)
    angle = azimuth + bi_ref[...].astype(F32) * (math.pi / 2.0)
    cosine = jnp.cos(angle)
    sine = jnp.sin(angle)
    x = bc_ref[:, 0, :]
    y = bc_ref[:, 1, :]
    pos[0] = cosine * x - sine * y
    pos[1] = sine * x + cosine * y
    pos[2] = bc_ref[:, 2, :]
    for s in range(steps):
        strength = bs_ref[s : s + 1, :]
        yparts[s] = split3(
            jnp.concatenate(
                [strength] + [strength * pos[c, s : s + 1, :] for c in range(3)], axis=0
            )
        )
    acc[...] = jnp.zeros_like(acc)

    pl.semaphore_wait(barrier, n * nb - 1)

    def offset(k):
        half = (k + 1) // 2
        return lax.rem(n + half * (2 * lax.rem(k, 2) - 1), n)

    def send_frame(k, _):
        other = lax.rem(me_f + n - offset(k), n)
        pltpu.make_async_remote_copy(
            src_ref=gath.at[0],
            dst_ref=gath.at[k],
            send_sem=g_send,
            recv_sem=g_recv.at[k],
            device_id=(other, me_b),
            device_id_type=MESH,
        ).start()
        return 0

    lax.fori_loop(1, n, send_frame, 0)

    for s in range(steps):
        for c in range(3):
            for j in range(width // LANES):
                piece = pos[c, s : s + 1, j * LANES : (j + 1) * LANES]
                spread[s * 3 + c, j * LANES : (j + 1) * LANES, :] = jnp.broadcast_to(
                    piece, (LANES, LANES)
                ).T

    def send_part(k, dest_f, dest_b, chunk):
        pltpu.make_async_remote_copy(
            src_ref=stage.at[k, chunk],
            dst_ref=land.at[k * nb + me_b],
            send_sem=p_send,
            recv_sem=p_recv,
            device_id=(dest_f, dest_b),
            device_id_type=MESH,
        ).start()

    def block(k, _):
        owner = lax.rem(me_f + offset(k), n)

        @pl.when(k > 0)
        def _():
            pltpu.make_async_copy(gath.at[k], gath.at[k], g_recv.at[k]).wait()

        fx = gath[k, 0:1, :]
        fy = gath[k, 1:2, :]
        fz = gath[k, 2:3, :]
        nx = gath[k, 3:4, :]
        ny = gath[k, 4:5, :]
        nz = gath[k, 5:6, :]
        fxb = jnp.broadcast_to(fx, (8, frame))
        fyb = jnp.broadcast_to(fy, (8, frame))
        fzb = jnp.broadcast_to(fz, (8, frame))
        fx16 = jnp.concatenate([fxb, fxb], axis=0)
        fy16 = jnp.concatenate([fyb, fyb], axis=0)
        fz16 = jnp.concatenate([fzb, fzb], axis=0)
        xs = []
        for s in range(steps):
            q = gath[k, 6 + s : 7 + s, :]
            xs.append(split3(jnp.concatenate([q, q * fx, q * fy, q * fz], axis=0)))
        over = (((1,), (1,)), ((), ()))
        pieces = [(s, i) for s in range(steps) for i in range(width // PIECE)]
        held = [[[[] for _ in range(frame // LANES)] for _ in range(2)] for _ in pieces]
        sums = [None] * steps
        back = [None] * steps

        def fill(p, part):
            s, i = pieces[p]
            each = PIECE // ROWS // 4
            for r in range(part * each, (part + 1) * each):
                lines = slice(r * ROWS, (r + 1) * ROWS)
                source = slice(i * PIECE + r * ROWS, i * PIECE + (r + 1) * ROWS)
                bx = spread[s * 3, source, :]
                by = spread[s * 3 + 1, source, :]
                bz = spread[s * 3 + 2, source, :]
                for h in range(frame // LANES):
                    cols = slice(h * LANES, (h + 1) * LANES)
                    dx = fx16[:, cols] - bx
                    dy = fy16[:, cols] - by
                    dz = fz16[:, cols] - bz
                    inv = lax.rsqrt(dx * dx + dy * dy + dz * dz + core_sq)
                    weight = inv * inv * inv
                    high = weight.astype(BF16)
                    held[p][0][h].append(high)
                    held[p][1][h].append((weight - high.astype(F32)).astype(BF16))

        def dots(p, part):
            s, i = pieces[p]
            source = slice(i * PIECE, (i + 1) * PIECE)
            weight = jnp.concatenate(
                [jnp.concatenate(tall, axis=0) for tall in held[p][part % 2]], axis=1
            )
            if part < 2:
                term = jnp.dot(yparts[s, :, source], weight, preferred_element_type=F32)
                sums[s] = term if sums[s] is None else sums[s] + term
            else:
                term = lax.dot_general(xs[s], weight, over, preferred_element_type=F32)
                if part == 2:
                    back[s] = term
                else:
                    acc[s, :, source] += back[s] + term

        for p in range(len(pieces) + 1):
            for part in range(4):
                if p < len(pieces):
                    fill(p, part)
                if p > 0:
                    dots(p - 1, part)
        out_rows = []
        for s in range(steps):
            total = fold3(sums[s])
            base = total[0:1]
            out_rows.append(
                kernel_scale
                * (
                    nx * (fx * base - total[1:2])
                    + ny * (fy * base - total[2:3])
                    + nz * (fz * base - total[3:4])
                )
            )
        part = jnp.concatenate(out_rows, axis=0)
        for h in range(frame // LANES):
            stage[k, h] = part[:, h * LANES : (h + 1) * LANES]

        @pl.when(k > 0)
        def _():
            for c in range(nb):
                send_part(k, owner, c, c // per_chunk)

        @pl.when(k == 0)
        def _():
            for d in range(1, nb):
                c = lax.rem(me_b + d, nb)
                send_part(0, me_f, c, c // per_chunk)

        return 0

    lax.fori_loop(0, n, block, 0)

    chunk = me_b // per_chunk
    land[me_b] = stage[0, chunk]

    for s in range(steps):
        sums = fold3(acc[s])
        for c in range(3):
            bv_ref[s, c : c + 1, :] = kernel_scale * (
                pos[c, s : s + 1, :] * sums[0:1] - sums[c + 1 : c + 2]
            )

    own = pl.ds(pl.multiple_of(chunk * LANES, LANES), LANES)
    onset_part = (
        an_ref[0:1, own] * on_ref[0] + an_ref[1:2, own] * on_ref[1] + an_ref[2:3, own] * on_ref[2]
    )
    extra = onset_part + 0.5 * aq_ref[:, own]

    rest = land.at[pl.ds(1, n * nb - 1)]
    pltpu.make_async_copy(rest, rest, p_recv).wait()
    total = jnp.sum(land[...], axis=0)
    resid = total + extra
    which = lax.rem(me_b, per_chunk)
    nv = total[:, 0:quarter]
    rv = resid[:, 0:quarter]
    for i in range(1, per_chunk):
        cols = slice(i * quarter, (i + 1) * quarter)
        nv = jnp.where(which == i, total[:, cols], nv)
        rv = jnp.where(which == i, resid[:, cols], rv)
    nv_ref[...] = nv
    rs_ref[...] = rv

    pltpu.make_async_copy(rest, rest, p_send).wait()
    blocks = gath.at[pl.ds(1, n - 1)]
    pltpu.make_async_copy(blocks, blocks, g_send).wait()


def body(n, nb, ac, an, aq, bc, bs, bi, az, onset):
    steps, _, width = bc.shape
    frame = ac.shape[1]
    quarter = frame // nb
    vmem = pl.BlockSpec(memory_space=pltpu.VMEM)
    smem = pl.BlockSpec(memory_space=pltpu.SMEM)
    return pl.pallas_call(
        functools.partial(kernel, n, nb),
        out_shape=(
            jax.ShapeDtypeStruct((steps, quarter), F32),
            jax.ShapeDtypeStruct((steps, 3, width), F32),
            jax.ShapeDtypeStruct((steps, quarter), F32),
        ),
        in_specs=[vmem] * 6 + [smem] * 2,
        out_specs=(vmem, vmem, vmem),
        scratch_shapes=[
            pltpu.VMEM((n, 16, frame), F32),
            pltpu.VMEM((steps * 3, width, LANES), F32),
            pltpu.VMEM((3, steps, width), F32),
            pltpu.VMEM((steps, 16, width), BF16),
            pltpu.VMEM((steps, 16, width), F32),
            pltpu.VMEM((n, frame // LANES, steps, LANES), F32),
            pltpu.VMEM((n * nb, steps, LANES), F32),
            pltpu.SemaphoreType.DMA,
            pltpu.SemaphoreType.DMA((n,)),
            pltpu.SemaphoreType.DMA,
            pltpu.SemaphoreType.DMA,
        ],
        compiler_params=pltpu.CompilerParams(
            collective_id=0, has_side_effects=True, vmem_limit_bytes=24 * 1024 * 1024
        ),
    )(ac, an, aq, bc, bs, bi.reshape(1, width), az, onset)


def solution(mesh):
    n = mesh.shape["fus"]
    nb = mesh.shape["blade"]
    both = ("fus", "blade")
    return jax.shard_map(
        functools.partial(body, n, nb),
        mesh=mesh,
        in_specs=(
            P(None, "fus"),
            P(None, "fus"),
            P(None, "fus"),
            P(None, None, both),
            P(None, both),
            P(both),
            P(),
            P(),
        ),
        out_specs=(P(None, both), P(None, None, both), P(None, both)),
        check_vma=False,
    )
```
